32 devices in a mesh: fsdp: 8 (over z, y), dp: 4 (over x, core).
Axes of the slice: x: 2, y: 2, z: 4, core: 2. Of those that a mesh axis runs over, the one named last changes fastest.
Arguments:
- tokens: bfloat16 [4, 1024, 8192], P('dp', 'fsdp'), may hold values from -6 to 6
- queries: bfloat16 [4, 1024, 4096], P('dp', 'fsdp'), may hold values from -40 to 40, as said below
- keys: bfloat16 [4, 1024, 512], P('dp', 'fsdp'), may hold values from -4 to 4
- memory: bfloat16 [4, 1024, 8192], P('dp', 'fsdp'), may hold values from -6 to 6
- mem_keys: bfloat16 [4, 1024, 512], P('dp', 'fsdp'), may hold values from -4 to 4
- cotangent: bfloat16 [4, 1024, 4096], P('dp', 'fsdp'), may hold values from -6 to 6
- value_weight: bfloat16 [8192, 512], P('fsdp'), may hold values from -0.0625 to 0.0625
- dest_group: int32 [4, 16], P('dp', 'fsdp'), may hold values from 0 to 3, as said below
- source_group: int32 [4, 16], P('dp', 'fsdp'), may hold values from 0 to 3, as said below
- lengths: int32 [4, 16], P('dp', 'fsdp'), may hold values from 1 to 64
Outputs:
- grad_queries: bfloat16 [4, 1024, 4096], P('dp', 'fsdp')
- grad_keys: bfloat16 [4, 1024, 512], P('dp', 'fsdp')
- grad_memory: bfloat16 [4, 1024, 8192], P('dp', 'fsdp')
- grad_mem_keys: bfloat16 [4, 1024, 512], P('dp', 'fsdp')
- grad_weight: bfloat16 [8192, 512], P('fsdp')
The draws below stay inside these ranges and needn't reach their ends.
Inputs may be any that keep to these rules, and one draw needn't show every extreme that they name: `queries`: large in the hidden draw where a query row copies its own key. `dest_group`: the 2 documents of a device go to two different groups, never its own; document k of every device of one fsdp index moves the same number of groups ahead. `source_group`: consistent with dest_group: every device receives exactly one document for each of its slots, at most one from each sender.
All inputs are finite; a program needn't handle non-finite values.
Results may differ from the reference program's by a relative error of at most 0.0075.
Values may be sent and summed in bfloat16 or wider, within the bound.
A program may use at most 128 MiB of HBM per device.

```python
import jax
import jax.numpy as jnp
from jax import lax

D = 8192
HEADS = 32
KV_HEADS = 4
HEAD_DIM = 128
SEG = 64
MEM = 64
SLOTS = 2
KVW = 512
QW = 4096
N_FSDP = 8
N_DP = 4


def key_draw(key):
    array_shape = (N_DP, N_FSDP * SLOTS * SEG, KV_HEADS * HEAD_DIM)
    normal_part = jax.random.normal(jax.random.fold_in(key, 11), array_shape, jnp.float32)
    return jnp.clip(normal_part, -4.0, 4.0)


def draw_keys(key, part):
    return key_draw(key).astype(jnp.bfloat16)


def draw_queries(key, part):
    row_total = N_FSDP * SLOTS * SEG
    array_shape = (N_DP, row_total, HEADS * HEAD_DIM)
    normal_part = jnp.clip(jax.random.normal(jax.random.fold_in(key, 21), array_shape, jnp.float32), -4.0, 4.0)
    return normal_part.astype(jnp.bfloat16)


def shift_table(key):
    first_shift = jax.random.randint(jax.random.fold_in(key, 5), (N_FSDP,), 1, N_DP)
    offset = jax.random.randint(jax.random.fold_in(key, 6), (N_FSDP,), 1, N_DP - 1)
    second_shift = 1 + (first_shift - 1 + offset) % (N_DP - 1)
    return jnp.stack([first_shift, second_shift], axis=1).astype(jnp.int32)


def draw_dest_group(key, part):
    shifts = shift_table(key)
    groups = jnp.arange(N_DP, dtype=jnp.int32)[:, None, None]
    return ((groups + shifts[None]) % N_DP).reshape(N_DP, N_FSDP * SLOTS).astype(jnp.int32)


def draw_source_group(key, part):
    shifts = shift_table(key)
    groups = jnp.arange(N_DP, dtype=jnp.int32)[:, None, None]
    return ((groups - shifts[None] + N_DP) % N_DP).reshape(N_DP, N_FSDP * SLOTS).astype(jnp.int32)


def plant(result, stream_key, least, largest):
    index_at = [jax.random.randint(jax.random.fold_in(stream_key, axis), (), 0, length) for axis, length in enumerate(result.shape)]
    main_axis = result.shape.index(max(result.shape))
    beside = index_at[:main_axis] + [(index_at[main_axis] + 1) % result.shape[main_axis]] + index_at[main_axis + 1:]
    return result.at[tuple(index_at)].set(least).at[tuple(beside)].set(largest)


def level_of(own_key, dims, split, low, largest):
    def one(dim, blocks):
        heights = jax.random.uniform(jax.random.fold_in(jax.random.fold_in(own_key, 6), dim), (blocks,), jnp.float32, low / len(split), largest / len(split))
        return jnp.repeat(jnp.exp(heights), dims[dim] // blocks).reshape((-1,) + (1,) * (len(dims) - dim - 1))

    level = one(*split[0])
    for cut in split[1:]:
        level = level * one(*cut)
    return level


def gaussian(key, shape, scale, bound, split=(), kind=jnp.bfloat16):
    entries = scale * jax.random.normal(key, shape, jnp.float32)
    if split:
        entries = entries * level_of(key, shape, split, -0.22, 0.18)
    return jnp.clip(entries, -bound, bound).astype(kind)


def setup_inputs(seed: int = 0) -> dict:
    seeds = jax.random.split(jax.random.key(seed), 11)
    tokens = gaussian(seeds[0], (N_DP, N_FSDP * SLOTS * SEG, D), 1.0, 6.0, ((0, 4), (1, 8)))
    queries = draw_queries(jax.random.fold_in(seeds[10], 71), 0)
    keys = draw_keys(jax.random.fold_in(seeds[10], 71), 0)
    memory = gaussian(seeds[3], (N_DP, N_FSDP * SLOTS * MEM, D), 1.0, 6.0, ((0, 4), (1, 8)))
    mem_keys = gaussian(seeds[4], (N_DP, N_FSDP * SLOTS * MEM, KVW), 1.0, 4.0, ((0, 4), (1, 8)))
    cotangent = gaussian(seeds[5], (N_DP, N_FSDP * SLOTS * SEG, QW), 1.0, 6.0, ((0, 4), (1, 8)))
    value_weight = gaussian(seeds[6], (D, KVW), D ** -0.5, 0.0625, ((0, 8),))
    dest_group = draw_dest_group(jax.random.fold_in(seeds[10], 71), 0)
    source_group = draw_source_group(jax.random.fold_in(seeds[10], 71), 0)
    lengths = plant(jax.random.randint(seeds[9], (N_DP, N_FSDP * SLOTS), 1, SEG + 1), jax.random.fold_in(seeds[9], 1), 1, SEG).astype(jnp.int32)
    return {"tokens": tokens, "queries": queries, "keys": keys, "memory": memory, "mem_keys": mem_keys, "cotangent": cotangent, "value_weight": value_weight, "dest_group": dest_group, "source_group": source_group, "lengths": lengths}


def round_low(array):
    return lax.optimization_barrier(array.astype(jnp.bfloat16)).astype(jnp.float32)


def attend(query_rows, seg_keys, seg_values, slot_keys, slot_values, upstream, length):
    seg_len = query_rows.shape[0]
    mem_len = slot_keys.shape[0]
    kv_width = seg_keys.shape[1]
    heads_kv = kv_width // HEAD_DIM
    group_size = query_rows.shape[1] // kv_width
    key_count = seg_len + mem_len
    all_keys = jnp.concatenate([slot_keys, seg_keys], axis=0).astype(jnp.float32).reshape(key_count, heads_kv, HEAD_DIM)
    all_values = jnp.concatenate([slot_values, seg_values], axis=0).astype(jnp.float32).reshape(key_count, heads_kv, HEAD_DIM)
    query_heads = query_rows.astype(jnp.float32).reshape(seg_len, heads_kv, group_size, HEAD_DIM)
    score_scale = HEAD_DIM ** -0.5
    scores = jnp.einsum("qkgd,jkd->kgqj", query_heads, all_keys) * score_scale
    positions = jnp.arange(seg_len)[:, None]
    columns = jnp.arange(key_count)[None, :]
    visible = (columns < mem_len) | (columns - mem_len <= positions)
    scores = jnp.where(visible, scores, -1e30)
    row_max = jnp.max(scores, axis=-1, keepdims=True)
    exp_scores = jnp.exp(scores - row_max)
    weights = exp_scores / jnp.sum(exp_scores, axis=-1, keepdims=True)
    weights_low = round_low(weights)
    output = round_low(jnp.einsum("kgqj,jkd->qkgd", weights_low, all_values))
    live_rows = (jnp.arange(seg_len) < length).astype(jnp.float32)
    masked = upstream.astype(jnp.float32).reshape(seg_len, heads_kv, group_size, HEAD_DIM) * live_rows[:, None, None, None]
    grad_weights = jnp.einsum("qkgd,jkd->kgqj", masked, all_values)
    grad_values = jnp.einsum("kgqj,qkgd->jkd", weights_low, masked).reshape(key_count, kv_width)
    row_delta = jnp.einsum("qkgd,qkgd->kgq", masked, output)
    grad_scores = round_low(weights * (grad_weights - row_delta[..., None]) * score_scale)
    grad_query = jnp.einsum("kgqj,jkd->qkgd", grad_scores, all_keys).reshape(seg_len, -1).astype(jnp.bfloat16)
    grad_all_keys = jnp.einsum("kgqj,qkgd->jkd", grad_scores, query_heads).reshape(key_count, kv_width)
    return grad_query, grad_all_keys[:mem_len], grad_all_keys[mem_len:], grad_values[:mem_len], grad_values[mem_len:]


def reference(tokens, queries, keys, memory, mem_keys, cotangent, value_weight, dest_group, source_group, lengths):
    kv_width = KV_HEADS * HEAD_DIM
    q_width = HEADS * HEAD_DIM
    token_flat = tokens.reshape(-1, D)
    memory_flat = memory.reshape(-1, D)
    seg_values = jnp.dot(token_flat, value_weight, preferred_element_type=jnp.float32).astype(jnp.bfloat16)
    mem_values = jnp.dot(memory_flat, value_weight, preferred_element_type=jnp.float32).astype(jnp.bfloat16)
    doc_shape = (N_DP, N_FSDP, SLOTS, MEM, kv_width)
    source_index = jnp.broadcast_to(source_group.reshape(N_DP, N_FSDP, SLOTS, 1, 1), doc_shape).astype(jnp.int32)
    slot_keys = jnp.take_along_axis(mem_keys.reshape(doc_shape), source_index, axis=0)
    slot_values = jnp.take_along_axis(mem_values.reshape(doc_shape), source_index, axis=0)
    blocks = N_DP * N_FSDP
    inputs = (queries.reshape(blocks, SLOTS, SEG, q_width),
              keys.reshape(blocks, SLOTS, SEG, kv_width),
              seg_values.reshape(blocks, SLOTS, SEG, kv_width),
              slot_keys.reshape(blocks, SLOTS, MEM, kv_width),
              slot_values.reshape(blocks, SLOTS, MEM, kv_width),
              cotangent.reshape(blocks, SLOTS, SEG, q_width),
              lengths.reshape(blocks, SLOTS))

    def one_block(pieces):
        return jax.vmap(attend)(*pieces)

    grad_query, slot_grad_keys, seg_grad_keys, slot_grad_values, seg_grad_values = lax.map(one_block, inputs)
    dest_index = jnp.broadcast_to(dest_group.reshape(N_DP, N_FSDP, SLOTS, 1, 1), doc_shape).astype(jnp.int32)
    back_keys = slot_grad_keys.astype(jnp.bfloat16).reshape(doc_shape)
    back_values = slot_grad_values.astype(jnp.bfloat16).reshape(doc_shape)
    doc_grad_keys = jnp.take_along_axis(back_keys, dest_index, axis=0)
    doc_grad_values = jnp.take_along_axis(back_values, dest_index, axis=0).reshape(-1, kv_width)
    grad_memory = jnp.dot(doc_grad_values, value_weight.T, preferred_element_type=jnp.float32).astype(jnp.bfloat16)
    seg_low = seg_grad_values.astype(jnp.bfloat16).reshape(-1, kv_width)
    grad_weight = jnp.dot(token_flat.T, seg_low, preferred_element_type=jnp.float32) + jnp.dot(memory_flat.T, doc_grad_values, preferred_element_type=jnp.float32)
    return (grad_query.reshape(N_DP, N_FSDP * SLOTS * SEG, q_width),
            seg_grad_keys.astype(jnp.bfloat16).reshape(N_DP, N_FSDP * SLOTS * SEG, kv_width),
            grad_memory.reshape(N_DP, N_FSDP * SLOTS * MEM, D),
            doc_grad_keys.reshape(N_DP, N_FSDP * SLOTS * MEM, kv_width),
            grad_weight.astype(jnp.bfloat16))
```

```python
import jax
import jax.numpy as jnp
from jax import lax
from jax.sharding import PartitionSpec as P

HEAD_DIM = 128
SCALE = HEAD_DIM ** (-0.5)
F32 = jnp.float32
BF16 = jnp.bfloat16


def softmax_part(query_heads, all_keys, masked):
    seg_len = query_heads.shape[0]
    key_count = all_keys.shape[0]
    mem_len = key_count - seg_len
    scores = jnp.einsum("qkgd,jkd->kgqj", query_heads, all_keys, preferred_element_type=F32) * SCALE
    positions = jnp.arange(seg_len)[:, None]
    columns = jnp.arange(key_count)[None, :]
    visible = (columns < mem_len) | (columns - mem_len <= positions)
    scores = jnp.where(visible, scores, -1e30)
    row_max = jnp.max(scores, axis=-1, keepdims=True)
    exp_scores = jnp.exp(scores - row_max)
    weights = exp_scores / jnp.sum(exp_scores, axis=-1, keepdims=True)
    weights_low = weights.astype(BF16)
    grad_values = jnp.einsum("kgqj,qkgd->jkd", weights_low, masked, preferred_element_type=F32)
    return weights, weights_low, grad_values.reshape(key_count, -1).astype(BF16)


def backward_part(query_heads, all_keys, all_values, masked, weights, weights_low):
    seg_len = query_heads.shape[0]
    key_count = all_keys.shape[0]
    output = jnp.einsum(
        "kgqj,jkd->qkgd", weights_low, all_values, preferred_element_type=F32
    ).astype(BF16)
    grad_weights = jnp.einsum("qkgd,jkd->kgqj", masked, all_values, preferred_element_type=F32)
    row_delta = jnp.einsum("qkgd,qkgd->kgq", masked, output, preferred_element_type=F32)
    grad_scores = (weights * (grad_weights - row_delta[..., None]) * SCALE).astype(BF16)
    grad_query = jnp.einsum("kgqj,jkd->qkgd", grad_scores, all_keys, preferred_element_type=F32)
    grad_keys = jnp.einsum("kgqj,qkgd->jkd", grad_scores, query_heads, preferred_element_type=F32)
    return (
        grad_query.reshape(seg_len, -1).astype(BF16),
        grad_keys.reshape(key_count, -1).astype(BF16),
    )


def pick(table, rows):
    shape = table.T.shape + (1,) * (rows.ndim - 1)
    return jnp.sum(jnp.where(table.T.reshape(shape), rows[None], 0), axis=1, dtype=rows.dtype)


def take(table, blocks):
    shape = table.shape + (1,) * (blocks.ndim - 1)
    return jnp.sum(jnp.where(table.reshape(shape), blocks[None], 0), axis=1, dtype=blocks.dtype)


def rotate(blocks, shift):
    groups = blocks.shape[0]
    return lax.dynamic_slice_in_dim(
        jnp.concatenate([blocks, blocks], axis=0), groups - shift, groups, axis=0
    )


def swap(blocks):
    return lax.all_to_all(blocks, "dp", split_axis=0, concat_axis=0, tiled=True)


def per_device(
    tokens, queries, keys, memory, mem_keys, cotangent, value_weight, dest_group, source_group, lengths
):
    groups = lax.axis_size("dp")
    shards = lax.axis_size("fsdp")
    me = lax.axis_index("dp")
    slots = dest_group.shape[1]
    seg_len = tokens.shape[1] // slots
    mem_len = memory.shape[1] // slots
    kv_width = value_weight.shape[1]
    width = tokens.shape[2]
    part = value_weight.shape[0] // groups
    seg_rows, mem_rows = slots * seg_len, slots * mem_len
    rows = seg_rows + mem_rows
    heads_kv = kv_width // HEAD_DIM
    group_size = queries.shape[2] // kv_width
    targets = jnp.arange(groups, dtype=jnp.int32)
    send_table = dest_group[0][:, None] == targets[None, :]
    take_table = source_group[0][:, None] == targets[None, :]
    shift = lax.rem(dest_group[0] - me + groups, groups)

    in_keys = swap(pick(send_table, mem_keys[0].reshape(slots, mem_len, kv_width)))
    weight_part = lax.all_gather(
        lax.dynamic_slice_in_dim(value_weight, me * part, part, axis=0), "fsdp", axis=0, tiled=True
    )
    stacked = jnp.concatenate([tokens[0], memory[0]], axis=0)
    stacked = stacked.reshape(rows, shards, groups, part).transpose(2, 0, 1, 3)
    stacked = swap(stacked.reshape(groups, rows, shards * part))

    slot_keys = take(take_table, in_keys)
    all_keys = jnp.concatenate([slot_keys, keys[0].reshape(slots, seg_len, kv_width)], axis=1)
    all_keys = all_keys.reshape(slots, mem_len + seg_len, heads_kv, HEAD_DIM)
    query_heads = queries[0].reshape(slots, seg_len, heads_kv, group_size, HEAD_DIM)
    live = (jnp.arange(seg_len)[None, :] < lengths[0][:, None]).astype(BF16)
    masked = cotangent[0].reshape(query_heads.shape) * live[:, :, None, None, None]
    weights, weights_low, grad_values = jax.vmap(softmax_part)(query_heads, all_keys, masked)

    own_grads = jnp.concatenate(
        [
            grad_values[:, mem_len:].reshape(seg_rows, kv_width),
            grad_values[:, :mem_len].reshape(mem_rows, kv_width),
        ],
        axis=0,
    )
    peer_grads = swap(jnp.broadcast_to(own_grads[None], (groups, rows, kv_width)))
    doc_grads = [
        rotate(
            peer_grads[:, seg_rows + k * mem_len : seg_rows + (k + 1) * mem_len],
            lax.rem(groups - shift[k], groups),
        )
        for k in range(slots)
    ]
    doc_grads = jnp.concatenate(doc_grads, axis=1)
    all_grads = jnp.concatenate([peer_grads[:, :seg_rows], doc_grads], axis=1)
    share = lax.dot_general(
        stacked.reshape(groups * rows, shards * part),
        all_grads.reshape(groups * rows, kv_width),
        (((0,), (0,)), ((), ())),
        preferred_element_type=F32,
    ).astype(BF16)
    share = lax.psum_scatter(share, "fsdp", scatter_dimension=0, tiled=True)
    grad_weight = lax.all_gather(share, "dp", axis=0, tiled=True)

    partial = jnp.dot(
        stacked.reshape(groups * rows, shards * part), weight_part, preferred_element_type=F32
    ).reshape(groups, rows, kv_width)
    routed = [partial[:, :seg_rows]] + [
        rotate(partial[:, seg_rows + k * mem_len : seg_rows + (k + 1) * mem_len], shift[k])
        for k in range(slots)
    ]
    values = jnp.sum(swap(jnp.concatenate(routed, axis=1)), axis=0).astype(BF16)
    all_values = jnp.concatenate(
        [
            values[seg_rows:].reshape(slots, mem_len, kv_width),
            values[:seg_rows].reshape(slots, seg_len, kv_width),
        ],
        axis=1,
    ).reshape(all_keys.shape)
    grad_query, grad_all_keys = jax.vmap(backward_part)(
        query_heads, all_keys, all_values, masked, weights, weights_low
    )
    doc_grad_keys = take(send_table, swap(pick(take_table, grad_all_keys[:, :mem_len])))

    grad_memory = lax.dot_general(
        doc_grads.reshape(groups * mem_rows, kv_width),
        weight_part,
        (((1,), (1,)), ((), ())),
        preferred_element_type=F32,
    ).astype(BF16)
    grad_memory = swap(grad_memory.reshape(groups, mem_rows, shards * part))
    grad_memory = grad_memory.reshape(groups, mem_rows, shards, part).transpose(1, 2, 0, 3)
    return (
        grad_query.reshape(1, seg_rows, -1),
        grad_all_keys[:, mem_len:].reshape(1, seg_rows, kv_width),
        grad_memory.reshape(1, mem_rows, width),
        doc_grad_keys.reshape(1, mem_rows, kv_width),
        grad_weight,
    )


def solution(mesh):
    rows = P("dp", "fsdp", None)
    table = P("dp", "fsdp")
    weight = P("fsdp", None)
    return jax.shard_map(
        per_device,
        mesh=mesh,
        in_specs=(rows,) * 6 + (weight, table, table, table),
        out_specs=(rows,) * 4 + (weight,),
        check_vma=False,
    )
```

```python
import jax
import jax.numpy as jnp
from jax import lax
from jax.experimental import pallas as pl
from jax.experimental.pallas import tpu as pltpu
from jax.sharding import PartitionSpec as P

HEAD_DIM = 128
SCALE = HEAD_DIM ** (-0.5)
F32 = jnp.float32
BF16 = jnp.bfloat16
MESH = pl.DeviceIdType.MESH


def mm(a, b, contract):
    return lax.dot_general(a, b, (contract, ((), ())), preferred_element_type=F32)


def stack_heads(ref, first_row, seg_len, kv, group_size):
    return jnp.concatenate(
        [
            ref[
                first_row : first_row + seg_len,
                (kv * group_size + j) * HEAD_DIM : (kv * group_size + j + 1) * HEAD_DIM,
            ]
            for j in range(group_size)
        ],
        axis=0,
    )


def head_inputs(q_ref, ct_ref, length, slot, kv, seg_len, mem_len, group_size):
    q = stack_heads(q_ref, slot * seg_len, seg_len, kv, group_size)
    u = stack_heads(ct_ref, slot * seg_len, seg_len, kv, group_size)
    shape = (group_size * seg_len, mem_len + seg_len)
    position = lax.rem(lax.broadcasted_iota(jnp.int32, shape, 0), seg_len)
    column = lax.broadcasted_iota(jnp.int32, shape, 1)
    visible = column - mem_len <= position
    row = lax.rem(lax.broadcasted_iota(jnp.int32, u.shape, 0), seg_len)
    u = jnp.where(row < length, u.astype(F32), 0.0).astype(BF16)
    return q, u, visible


def softmax(q, k, visible):
    scores = jnp.where(visible, mm(q, k, ((1,), (1,))) * SCALE, -1e30)
    exp_scores = jnp.exp(scores - jnp.max(scores, axis=-1, keepdims=True))
    return exp_scores / jnp.sum(exp_scores, axis=-1, keepdims=True)


def forward_kernel(
    tokens, memory, weight, mem_keys, queries, keys, cotangent, source, lengths,
    x_out, w_out, g_out, k_out,
    peer_keys, own_grads,
    x_send, x_recv, w_send, w_recv, k_send, k_recv, g_send, g_recv, local_sem,
):
    groups, shards = lax.axis_size("dp"), lax.axis_size("fsdp")
    me, idx = lax.axis_index("dp"), lax.axis_index("fsdp")
    seg_rows, mem_rows = tokens.shape[0], memory.shape[0]
    slots = lengths.shape[1]
    seg_len, mem_len = seg_rows // slots, mem_rows // slots
    depth, kv_width = weight.shape
    part = depth // groups
    group_size = queries.shape[1] // kv_width

    barrier = pltpu.get_barrier_semaphore()
    for d in range(1, groups):
        pl.semaphore_signal(
            barrier, 1, device_id={"dp": lax.rem(me + d, groups)}, device_id_type=MESH
        )

    @pl.loop(1, shards)
    def _(d):
        pl.semaphore_signal(
            barrier, 1, device_id={"fsdp": lax.rem(idx + d, shards)}, device_id_type=MESH
        )

    pl.semaphore_wait(barrier, groups + shards - 2)

    def key_copy(d):
        return pltpu.make_async_remote_copy(
            mem_keys, peer_keys.at[me], k_send.at[d], k_recv.at[d],
            device_id={"dp": lax.rem(me + d, groups)}, device_id_type=MESH,
        )

    for d in range(1, groups):
        key_copy(d).start()

    w_src = weight.at[pl.ds(pl.multiple_of(me * part, 16), part)]

    def weight_copy(d):
        return pltpu.make_async_remote_copy(
            w_src, w_out.at[pl.ds(pl.multiple_of(idx * part, 16), part)], w_send.at[d], w_recv.at[d],
            device_id={"fsdp": lax.rem(idx + d, shards)}, device_id_type=MESH,
        )

    @pl.loop(1, shards)
    def _(d):
        weight_copy(d).start()

    def source_block(ref, target, block):
        return ref.at[:, pl.ds(pl.multiple_of(block * depth + target * part, 128), part)]

    def x_block(first, count, block):
        return x_out.at[me, pl.ds(first, count), pl.ds(pl.multiple_of(block * part, 128), part)]

    pieces = ((tokens, 0, seg_rows), (memory, seg_rows, mem_rows))

    @pl.loop(0, shards)
    def _(block):
        for d in range(1, groups):
            target = lax.rem(me + d, groups)
            for ref, first, count in pieces:
                pltpu.make_async_remote_copy(
                    source_block(ref, target, block), x_block(first, count, block),
                    x_send.at[d], x_recv.at[d],
                    device_id={"dp": target}, device_id_type=MESH,
                ).start()
        for ref, first, count in pieces:
            pltpu.make_async_copy(
                source_block(ref, me, block), x_block(first, count, block), local_sem.at[0]
            ).start()

    own_weight = pltpu.make_async_copy(
        w_src, w_out.at[pl.ds(pl.multiple_of(idx * part, 16), part)], local_sem.at[1]
    )
    own_weight.start()
    peer_keys[me] = mem_keys[...]
    for d in range(1, groups):
        key_copy(d).wait_recv()

    for slot in range(slots):
        k_out[slot, :mem_len, :] = peer_keys[
            source[0, slot], slot * mem_len : (slot + 1) * mem_len, :
        ]
        k_out[slot, mem_len:, :] = keys[slot * seg_len : (slot + 1) * seg_len, :]
        for kv in range(kv_width // HEAD_DIM):
            lanes = slice(kv * HEAD_DIM, (kv + 1) * HEAD_DIM)
            q, u, visible = head_inputs(
                queries, cotangent, lengths[0, slot], slot, kv, seg_len, mem_len, group_size
            )
            probs = softmax(q, k_out[slot, :, lanes], visible).astype(BF16)
            grads = mm(probs, u, ((0,), (0,))).astype(BF16)
            own_grads[slot * seg_len : (slot + 1) * seg_len, lanes] = grads[mem_len:]
            own_grads[seg_rows + slot * mem_len : seg_rows + (slot + 1) * mem_len, lanes] = grads[
                :mem_len
            ]

    def grad_copy(d):
        return pltpu.make_async_remote_copy(
            own_grads, g_out.at[me], g_send.at[d], g_recv.at[d],
            device_id={"dp": lax.rem(me + d, groups)}, device_id_type=MESH,
        )

    for d in range(1, groups):
        grad_copy(d).start()
    own = pltpu.make_async_copy(own_grads, g_out.at[me], local_sem.at[2])
    own.start()
    own.wait()
    own_weight.wait()
    pltpu.make_async_copy(x_out.at[me], x_out.at[me], local_sem.at[0]).wait()
    for d in range(1, groups):
        key_copy(d).wait_send()
        grad_copy(d).wait()
        whole = pltpu.make_async_remote_copy(
            x_out.at[me], x_out.at[me], x_send.at[d], x_recv.at[d],
            device_id={"dp": lax.rem(me + d, groups)}, device_id_type=MESH,
        )
        whole.wait()

    @pl.loop(1, shards)
    def _(d):
        weight_copy(d).wait()


def run_forward(groups, shards, tokens, memory, weight, mem_keys, queries, keys, cotangent, source, lengths):
    rows = tokens.shape[0] + memory.shape[0]
    depth, kv_width = weight.shape
    width = tokens.shape[1] // groups
    slots = lengths.shape[1]
    any_spec = pl.BlockSpec(memory_space=pl.ANY)
    vmem = pl.BlockSpec(memory_space=pltpu.VMEM)
    smem = pl.BlockSpec(memory_space=pltpu.SMEM)
    dma = pltpu.SemaphoreType.DMA
    return pl.pallas_call(
        forward_kernel,
        out_shape=(
            jax.ShapeDtypeStruct((groups, rows, width), BF16),
            jax.ShapeDtypeStruct((width, kv_width), BF16),
            jax.ShapeDtypeStruct((groups, rows, kv_width), BF16),
            jax.ShapeDtypeStruct((slots, rows // slots, kv_width), BF16),
        ),
        in_specs=[any_spec] * 3 + [vmem] * 4 + [smem] * 2,
        out_specs=(any_spec, any_spec, any_spec, vmem),
        scratch_shapes=[
            pltpu.VMEM((groups, memory.shape[0], kv_width), BF16),
            pltpu.VMEM((rows, kv_width), BF16),
            dma((groups,)), dma((groups,)), dma((shards,)), dma((shards,)),
            dma((groups,)), dma((groups,)), dma((groups,)), dma((groups,)), dma((3,)),
        ],
        compiler_params=pltpu.CompilerParams(
            collective_id=0, has_side_effects=True, vmem_limit_bytes=40 * 2**20
        ),
        name="forward",
    )(tokens, memory, weight, mem_keys, queries, keys, cotangent, source, lengths)


def backward_kernel(queries, all_keys, cotangent, values, lengths, gq_out, gk_out):
    slots, key_count, kv_width = all_keys.shape
    seg_rows = queries.shape[0]
    seg_len = seg_rows // slots
    mem_len = key_count - seg_len
    group_size = queries.shape[1] // kv_width
    for slot in range(slots):
        for kv in range(kv_width // HEAD_DIM):
            lanes = slice(kv * HEAD_DIM, (kv + 1) * HEAD_DIM)
            q, u, visible = head_inputs(
                queries, cotangent, lengths[0, slot], slot, kv, seg_len, mem_len, group_size
            )
            k = all_keys[slot, :, lanes]
            v = jnp.concatenate(
                [
                    values[seg_rows + slot * mem_len : seg_rows + (slot + 1) * mem_len, lanes],
                    values[slot * seg_len : (slot + 1) * seg_len, lanes],
                ],
                axis=0,
            )
            probs = softmax(q, k, visible)
            attn = mm(probs.astype(BF16), v, ((1,), (0,))).astype(BF16)
            grad_probs = mm(u, v, ((1,), (1,)))
            delta = jnp.sum(u.astype(F32) * attn.astype(F32), axis=-1, keepdims=True)
            grad_scores = (probs * (grad_probs - delta) * SCALE).astype(BF16)
            grad_q = mm(grad_scores, k, ((1,), (0,))).astype(BF16)
            for j in range(group_size):
                at = (kv * group_size + j) * HEAD_DIM
                gq_out[slot * seg_len : (slot + 1) * seg_len, at : at + HEAD_DIM] = grad_q[
                    j * seg_len : (j + 1) * seg_len
                ]
            gk_out[slot, :, lanes] = mm(grad_scores, q, ((0,), (0,))).astype(BF16)


def run_backward(queries, all_keys, cotangent, values, lengths):
    vmem = pl.BlockSpec(memory_space=pltpu.VMEM)
    return pl.pallas_call(
        backward_kernel,
        out_shape=(
            jax.ShapeDtypeStruct(queries.shape, BF16),
            jax.ShapeDtypeStruct(all_keys.shape, BF16),
        ),
        in_specs=[vmem] * 4 + [pl.BlockSpec(memory_space=pltpu.SMEM)],
        out_specs=(vmem, vmem),
        compiler_params=pltpu.CompilerParams(vmem_limit_bytes=40 * 2**20),
        cost_estimate=pl.CostEstimate(flops=10**9, bytes_accessed=8 * 2**20, transcendentals=10**6),
        name="backward",
    )(queries, all_keys, cotangent, values, lengths)


def pick(table, rows):
    shape = table.T.shape + (1,) * (rows.ndim - 1)
    return jnp.sum(jnp.where(table.T.reshape(shape), rows[None], 0), axis=1, dtype=rows.dtype)


def take(table, blocks):
    shape = table.shape + (1,) * (blocks.ndim - 1)
    return jnp.sum(jnp.where(table.reshape(shape), blocks[None], 0), axis=1, dtype=blocks.dtype)


def rotate(blocks, shift):
    groups = blocks.shape[0]
    return lax.dynamic_slice_in_dim(
        jnp.concatenate([blocks, blocks], axis=0), groups - shift, groups, axis=0
    )


def swap(blocks):
    return lax.all_to_all(blocks, "dp", split_axis=0, concat_axis=0, tiled=True)


def softmax_part(query_heads, all_keys, masked):
    seg_len = query_heads.shape[0]
    key_count = all_keys.shape[0]
    mem_len = key_count - seg_len
    scores = jnp.einsum("qkgd,jkd->kgqj", query_heads, all_keys, preferred_element_type=F32) * SCALE
    positions = jnp.arange(seg_len)[:, None]
    columns = jnp.arange(key_count)[None, :]
    visible = (columns < mem_len) | (columns - mem_len <= positions)
    scores = jnp.where(visible, scores, -1e30)
    row_max = jnp.max(scores, axis=-1, keepdims=True)
    exp_scores = jnp.exp(scores - row_max)
    weights = exp_scores / jnp.sum(exp_scores, axis=-1, keepdims=True)
    weights_low = weights.astype(BF16)
    grad_values = jnp.einsum("kgqj,qkgd->jkd", weights_low, masked, preferred_element_type=F32)
    return weights, weights_low, grad_values.reshape(key_count, -1).astype(BF16)


def plain_forward(
    groups, shards, tokens, memory, weight, mem_keys, queries, keys, cotangent,
    send_table, take_table, lengths,
):
    me = lax.axis_index("dp")
    slots = lengths.shape[1]
    seg_rows, mem_rows = tokens.shape[0], memory.shape[0]
    rows = seg_rows + mem_rows
    seg_len, mem_len = seg_rows // slots, mem_rows // slots
    depth, kv_width = weight.shape
    part = depth // groups
    heads_kv = kv_width // HEAD_DIM
    group_size = queries.shape[1] // kv_width
    in_keys = swap(pick(send_table, mem_keys.reshape(slots, mem_len, kv_width)))
    weight_part = lax.all_gather(
        lax.dynamic_slice_in_dim(weight, me * part, part, axis=0), "fsdp", axis=0, tiled=True
    )
    stacked = jnp.concatenate([tokens, memory], axis=0)
    stacked = stacked.reshape(rows, shards, groups, part).transpose(2, 0, 1, 3)
    stacked = swap(stacked.reshape(groups, rows, shards * part))

    slot_keys = take(take_table, in_keys)
    all_keys = jnp.concatenate([slot_keys, keys.reshape(slots, seg_len, kv_width)], axis=1)
    all_keys = all_keys.reshape(slots, mem_len + seg_len, heads_kv, HEAD_DIM)
    query_heads = queries.reshape(slots, seg_len, heads_kv, group_size, HEAD_DIM)
    live = (jnp.arange(seg_len)[None, :] < lengths[0][:, None]).astype(BF16)
    masked = cotangent.reshape(query_heads.shape) * live[:, :, None, None, None]
    weights, weights_low, grad_values = jax.vmap(softmax_part)(query_heads, all_keys, masked)

    own_grads = jnp.concatenate(
        [
            grad_values[:, mem_len:].reshape(seg_rows, kv_width),
            grad_values[:, :mem_len].reshape(mem_rows, kv_width),
        ],
        axis=0,
    )
    peer_grads = swap(jnp.broadcast_to(own_grads[None], (groups, rows, kv_width)))
    return stacked, weight_part, peer_grads, all_keys.reshape(slots, -1, kv_width)


def per_device(
    tokens, queries, keys, memory, mem_keys, cotangent, value_weight, dest_group, source_group, lengths
):
    groups = lax.axis_size("dp")
    shards = lax.axis_size("fsdp")
    me = lax.axis_index("dp")
    slots = dest_group.shape[1]
    seg_len = tokens.shape[1] // slots
    mem_len = memory.shape[1] // slots
    kv_width = value_weight.shape[1]
    width = tokens.shape[2]
    part = value_weight.shape[0] // groups
    seg_rows, mem_rows = slots * seg_len, slots * mem_len
    rows = seg_rows + mem_rows
    targets = jnp.arange(groups, dtype=jnp.int32)
    send_table = dest_group[0][:, None] == targets[None, :]
    take_table = source_group[0][:, None] == targets[None, :]
    shift = lax.rem(dest_group[0] - me + groups, groups)

    arrays = (tokens[0], memory[0], value_weight, mem_keys[0], queries[0], keys[0], cotangent[0])
    if part % 128:
        forward = plain_forward(groups, shards, *arrays, send_table, take_table, lengths)
    else:
        forward = run_forward(groups, shards, *arrays, source_group, lengths)
    stacked, weight_part, peer_grads, all_keys = forward
    doc_grads = [
        rotate(
            peer_grads[:, seg_rows + k * mem_len : seg_rows + (k + 1) * mem_len],
            lax.rem(groups - shift[k], groups),
        )
        for k in range(slots)
    ]
    doc_grads = jnp.concatenate(doc_grads, axis=1)
    all_grads = jnp.concatenate([peer_grads[:, :seg_rows], doc_grads], axis=1)
    share = lax.dot_general(
        stacked.reshape(groups * rows, shards * part),
        all_grads.reshape(groups * rows, kv_width),
        (((0,), (0,)), ((), ())),
        preferred_element_type=F32,
    ).astype(BF16)
    share = lax.psum_scatter(share, "fsdp", scatter_dimension=0, tiled=True)
    grad_weight = lax.all_gather(share, "dp", axis=0, tiled=True)

    partial = jnp.dot(
        stacked.reshape(groups * rows, shards * part), weight_part, preferred_element_type=F32
    ).reshape(groups, rows, kv_width)
    routed = [partial[:, :seg_rows]] + [
        rotate(partial[:, seg_rows + k * mem_len : seg_rows + (k + 1) * mem_len], shift[k])
        for k in range(slots)
    ]
    values = jnp.sum(swap(jnp.concatenate(routed, axis=1)), axis=0).astype(BF16)
    grad_query, grad_all_keys = run_backward(queries[0], all_keys, cotangent[0], values, lengths)
    doc_grad_keys = take(send_table, swap(pick(take_table, grad_all_keys[:, :mem_len])))

    grad_memory = lax.dot_general(
        doc_grads.reshape(groups * mem_rows, kv_width),
        weight_part,
        (((1,), (1,)), ((), ())),
        preferred_element_type=F32,
    ).astype(BF16)
    grad_memory = swap(grad_memory.reshape(groups, mem_rows, shards * part))
    grad_memory = grad_memory.reshape(groups, mem_rows, shards, part).transpose(1, 2, 0, 3)
    return (
        grad_query[None],
        grad_all_keys[:, mem_len:].reshape(1, seg_rows, kv_width),
        grad_memory.reshape(1, mem_rows, width),
        doc_grad_keys.reshape(1, mem_rows, kv_width),
        grad_weight,
    )


def solution(mesh):
    rows = P("dp", "fsdp", None)
    table = P("dp", "fsdp")
    weight = P("fsdp", None)
    return jax.shard_map(
        per_device,
        mesh=mesh,
        in_specs=(rows,) * 6 + (weight, table, table, table),
        out_specs=(rows,) * 4 + (weight,),
        check_vma=False,
    )
```

```python
import jax
import jax.numpy as jnp
from jax import lax
from jax.experimental import pallas as pl
from jax.experimental.pallas import tpu as pltpu
from jax.sharding import PartitionSpec as P

HEAD_DIM = 128
SCALE = HEAD_DIM ** (-0.5)
F32 = jnp.float32
BF16 = jnp.bfloat16
MESH = pl.DeviceIdType.MESH


def mm(a, b, contract):
    return lax.dot_general(a, b, (contract, ((), ())), preferred_element_type=F32)


def stack_heads(ref, first_row, seg_len, kv, group_size):
    return jnp.concatenate(
        [
            ref[
                first_row : first_row + seg_len,
                (kv * group_size + j) * HEAD_DIM : (kv * group_size + j + 1) * HEAD_DIM,
            ]
            for j in range(group_size)
        ],
        axis=0,
    )


def head_inputs(q_ref, ct_ref, length, slot, kv, seg_len, mem_len, group_size):
    q = stack_heads(q_ref, slot * seg_len, seg_len, kv, group_size)
    u = stack_heads(ct_ref, slot * seg_len, seg_len, kv, group_size)
    shape = (group_size * seg_len, mem_len + seg_len)
    position = lax.rem(lax.broadcasted_iota(jnp.int32, shape, 0), seg_len)
    column = lax.broadcasted_iota(jnp.int32, shape, 1)
    visible = column - mem_len <= position
    row = lax.rem(lax.broadcasted_iota(jnp.int32, u.shape, 0), seg_len)
    u = jnp.where(row < length, u.astype(F32), 0.0).astype(BF16)
    return q, u, visible


def softmax(q, k, visible):
    scores = jnp.where(visible, mm(q, k, ((1,), (1,))) * SCALE, -1e30)
    exp_scores = jnp.exp(scores - jnp.max(scores, axis=-1, keepdims=True))
    return exp_scores / jnp.sum(exp_scores, axis=-1, keepdims=True)


def forward_kernel(
    tokens, memory, weight, mem_keys, queries, keys, cotangent, source, lengths,
    x_out, w_out, g_out, k_out,
    peer_keys, own_grads,
    x_send, x_recv, w_send, w_recv, k_send, k_recv, g_send, g_recv, local_sem,
):
    groups, shards = lax.axis_size("dp"), lax.axis_size("fsdp")
    me, idx = lax.axis_index("dp"), lax.axis_index("fsdp")
    seg_rows, mem_rows = tokens.shape[0], memory.shape[0]
    slots = lengths.shape[1]
    seg_len, mem_len = seg_rows // slots, mem_rows // slots
    depth, kv_width = weight.shape
    part = depth // groups
    group_size = queries.shape[1] // kv_width

    barrier = pltpu.get_barrier_semaphore()
    for d in range(1, groups):
        pl.semaphore_signal(
            barrier, 1, device_id={"dp": lax.rem(me + d, groups)}, device_id_type=MESH
        )

    @pl.loop(1, shards)
    def _(d):
        pl.semaphore_signal(
            barrier, 1, device_id={"fsdp": lax.rem(idx + d, shards)}, device_id_type=MESH
        )

    pl.semaphore_wait(barrier, groups + shards - 2)

    def key_copy(d):
        return pltpu.make_async_remote_copy(
            mem_keys, peer_keys.at[me], k_send.at[d], k_recv.at[d],
            device_id={"dp": lax.rem(me + d, groups)}, device_id_type=MESH,
        )

    for d in range(1, groups):
        key_copy(d).start()

    w_src = weight.at[pl.ds(pl.multiple_of(me * part, 16), part)]

    def weight_copy(d):
        return pltpu.make_async_remote_copy(
            w_src, w_out.at[pl.ds(pl.multiple_of(idx * part, 16), part)], w_send.at[d], w_recv.at[d],
            device_id={"fsdp": lax.rem(idx + d, shards)}, device_id_type=MESH,
        )

    @pl.loop(1, shards)
    def _(d):
        weight_copy(d).start()

    def source_block(ref, target, block):
        return ref.at[:, pl.ds(pl.multiple_of(block * depth + target * part, 128), part)]

    def x_block(first, count, block):
        return x_out.at[me, pl.ds(first, count), pl.ds(pl.multiple_of(block * part, 128), part)]

    pieces = ((tokens, 0, seg_rows), (memory, seg_rows, mem_rows))

    @pl.loop(0, shards)
    def _(block):
        for d in range(1, groups):
            target = lax.rem(me + d, groups)
            for ref, first, count in pieces:
                pltpu.make_async_remote_copy(
                    source_block(ref, target, block), x_block(first, count, block),
                    x_send.at[d], x_recv.at[d],
                    device_id={"dp": target}, device_id_type=MESH,
                ).start()
        for ref, first, count in pieces:
            pltpu.make_async_copy(
                source_block(ref, me, block), x_block(first, count, block), local_sem.at[0]
            ).start()

    own_weight = pltpu.make_async_copy(
        w_src, w_out.at[pl.ds(pl.multiple_of(idx * part, 16), part)], local_sem.at[1]
    )
    own_weight.start()
    peer_keys[me] = mem_keys[...]
    for d in range(1, groups):
        key_copy(d).wait_recv()

    for slot in range(slots):
        k_out[slot, :mem_len, :] = peer_keys[
            source[0, slot], slot * mem_len : (slot + 1) * mem_len, :
        ]
        k_out[slot, mem_len:, :] = keys[slot * seg_len : (slot + 1) * seg_len, :]
        for kv in range(kv_width // HEAD_DIM):
            lanes = slice(kv * HEAD_DIM, (kv + 1) * HEAD_DIM)
            q, u, visible = head_inputs(
                queries, cotangent, lengths[0, slot], slot, kv, seg_len, mem_len, group_size
            )
            probs = softmax(q, k_out[slot, :, lanes], visible).astype(BF16)
            grads = mm(probs, u, ((0,), (0,))).astype(BF16)
            own_grads[slot * seg_len : (slot + 1) * seg_len, lanes] = grads[mem_len:]
            own_grads[seg_rows + slot * mem_len : seg_rows + (slot + 1) * mem_len, lanes] = grads[
                :mem_len
            ]

    def grad_copy(d):
        return pltpu.make_async_remote_copy(
            own_grads, g_out.at[me], g_send.at[d], g_recv.at[d],
            device_id={"dp": lax.rem(me + d, groups)}, device_id_type=MESH,
        )

    for d in range(1, groups):
        grad_copy(d).start()
    own = pltpu.make_async_copy(own_grads, g_out.at[me], local_sem.at[2])
    own.start()
    own.wait()
    own_weight.wait()
    pltpu.make_async_copy(x_out.at[me], x_out.at[me], local_sem.at[0]).wait()
    for d in range(1, groups):
        key_copy(d).wait_send()
        grad_copy(d).wait()
        whole = pltpu.make_async_remote_copy(
            x_out.at[me], x_out.at[me], x_send.at[d], x_recv.at[d],
            device_id={"dp": lax.rem(me + d, groups)}, device_id_type=MESH,
        )
        whole.wait()

    @pl.loop(1, shards)
    def _(d):
        weight_copy(d).wait()


def run_forward(groups, shards, tokens, memory, weight, mem_keys, queries, keys, cotangent, source, lengths):
    rows = tokens.shape[0] + memory.shape[0]
    depth, kv_width = weight.shape
    width = tokens.shape[1] // groups
    slots = lengths.shape[1]
    any_spec = pl.BlockSpec(memory_space=pl.ANY)
    vmem = pl.BlockSpec(memory_space=pltpu.VMEM)
    smem = pl.BlockSpec(memory_space=pltpu.SMEM)
    dma = pltpu.SemaphoreType.DMA
    return pl.pallas_call(
        forward_kernel,
        out_shape=(
            jax.ShapeDtypeStruct((groups, rows, width), BF16),
            jax.ShapeDtypeStruct((width, kv_width), BF16),
            jax.ShapeDtypeStruct((groups, rows, kv_width), BF16),
            jax.ShapeDtypeStruct((slots, rows // slots, kv_width), BF16),
        ),
        in_specs=[any_spec] * 3 + [vmem] * 4 + [smem] * 2,
        out_specs=(any_spec, any_spec, any_spec, vmem),
        scratch_shapes=[
            pltpu.VMEM((groups, memory.shape[0], kv_width), BF16),
            pltpu.VMEM((rows, kv_width), BF16),
            dma((groups,)), dma((groups,)), dma((shards,)), dma((shards,)),
            dma((groups,)), dma((groups,)), dma((groups,)), dma((groups,)), dma((3,)),
        ],
        compiler_params=pltpu.CompilerParams(
            collective_id=0, has_side_effects=True, vmem_limit_bytes=40 * 2**20
        ),
        name="forward",
    )(tokens, memory, weight, mem_keys, queries, keys, cotangent, source, lengths)


def attention_backward(queries, all_keys, cotangent, values, lengths, gq_out, gk_out, gmk_out):
    slots, key_count, kv_width = all_keys.shape
    seg_rows = queries.shape[0]
    seg_len = seg_rows // slots
    mem_len = key_count - seg_len
    group_size = queries.shape[1] // kv_width
    for slot in range(slots):
        for kv in range(kv_width // HEAD_DIM):
            lanes = slice(kv * HEAD_DIM, (kv + 1) * HEAD_DIM)
            q, u, visible = head_inputs(
                queries, cotangent, lengths[0, slot], slot, kv, seg_len, mem_len, group_size
            )
            k = all_keys[slot, :, lanes]
            v = jnp.concatenate(
                [
                    values[seg_rows + slot * mem_len : seg_rows + (slot + 1) * mem_len, lanes],
                    values[slot * seg_len : (slot + 1) * seg_len, lanes],
                ],
                axis=0,
            )
            probs = softmax(q, k, visible)
            attn = mm(probs.astype(BF16), v, ((1,), (0,))).astype(BF16)
            grad_probs = mm(u, v, ((1,), (1,)))
            delta = jnp.sum(u.astype(F32) * attn.astype(F32), axis=-1, keepdims=True)
            grad_scores = (probs * (grad_probs - delta) * SCALE).astype(BF16)
            grad_q = mm(grad_scores, k, ((1,), (0,))).astype(BF16)
            for j in range(group_size):
                at = (kv * group_size + j) * HEAD_DIM
                gq_out[slot * seg_len : (slot + 1) * seg_len, at : at + HEAD_DIM] = grad_q[
                    j * seg_len : (j + 1) * seg_len
                ]
            grad_k = mm(grad_scores, q, ((0,), (0,))).astype(BF16)
            gk_out[slot * seg_len : (slot + 1) * seg_len, lanes] = grad_k[mem_len:]
            gmk_out[slot * mem_len : (slot + 1) * mem_len, lanes] = grad_k[:mem_len]


def run_backward(queries, all_keys, cotangent, values, lengths):
    vmem = pl.BlockSpec(memory_space=pltpu.VMEM)
    return pl.pallas_call(
        attention_backward,
        out_shape=(
            jax.ShapeDtypeStruct(queries.shape, BF16),
            jax.ShapeDtypeStruct((queries.shape[0], all_keys.shape[2]), BF16),
            jax.ShapeDtypeStruct((values.shape[0] - queries.shape[0], all_keys.shape[2]), BF16),
        ),
        in_specs=[vmem] * 4 + [pl.BlockSpec(memory_space=pltpu.SMEM)],
        out_specs=(vmem, vmem, vmem),
        compiler_params=pltpu.CompilerParams(vmem_limit_bytes=40 * 2**20),
        cost_estimate=pl.CostEstimate(flops=10**9, bytes_accessed=8 * 2**20, transcendentals=10**6),
        name="backward",
    )(queries, all_keys, cotangent, values, lengths)


def tail_kernel(
    x, w, grads, queries, all_keys, cotangent, dest, lengths,
    gq_out, gk_out, gm_out, gmk_out, gw_out,
    aligned, routed, v_own, v_buf, v_in, values, s_own, s_buf, s_in, m_buf, mem_grads, k_in,
    v_send, v_recv, s_send, s_recv, m_send, m_recv, k_send, k_recv, f_send, f_recv,
):
    groups, shards = lax.axis_size("dp"), lax.axis_size("fsdp")
    me, idx = lax.axis_index("dp"), lax.axis_index("fsdp")
    slots, key_count, kv_width = all_keys.shape
    seg_rows = queries.shape[0]
    rows = x.shape[1]
    mem_rows = rows - seg_rows
    seg_len, mem_len = seg_rows // slots, mem_rows // slots
    part = gw_out.shape[0] // groups
    depth = part * groups

    barrier = pltpu.get_barrier_semaphore()
    for d in range(1, groups):
        pl.semaphore_signal(
            barrier, 1, device_id={"dp": lax.rem(me + d, groups)}, device_id_type=MESH
        )

    @pl.loop(1, shards)
    def _(d):
        pl.semaphore_signal(
            barrier, 1, device_id={"fsdp": lax.rem(idx + d, shards)}, device_id_type=MESH
        )

    pl.semaphore_wait(barrier, groups + shards - 2)

    def to_group(d, src, dst, send, recv):
        return pltpu.make_async_remote_copy(
            src, dst, send.at[d], recv.at[d],
            device_id={"dp": lax.rem(me + d, groups)}, device_id_type=MESH,
        )

    shifts = [lax.rem(dest[0, k] - me + groups, groups) for k in range(slots)]

    def value_part(d):
        target = lax.rem(me + d, groups)
        routed[:seg_rows, :] = x[target, :seg_rows, :]
        for k in range(slots):
            at = slice(seg_rows + k * mem_len, seg_rows + (k + 1) * mem_len)
            routed[at, :] = x[lax.rem(target - shifts[k] + groups, groups), at, :]
        return mm(routed[...], w[...], ((1,), (0,)))

    def value_copy(d):
        return to_group(d, v_buf.at[d], v_in.at[d], v_send, v_recv)

    for d in range(1, groups):
        v_buf[d] = value_part(d)
        value_copy(d).start()

    for g in range(groups):
        aligned[g * rows : g * rows + seg_rows, :] = grads[g, :seg_rows, :]
        for k in range(slots):
            at = slice(seg_rows + k * mem_len, seg_rows + (k + 1) * mem_len)
            aligned[g * rows + at.start : g * rows + at.stop, :] = grads[
                lax.rem(g + shifts[k], groups), at, :
            ]

    def weight_share(d):
        lanes = pl.ds(pl.multiple_of(lax.rem(idx + d, shards) * part, 128), part)
        total = mm(x[0, :, lanes], aligned[:rows, :], ((0,), (0,)))
        for g in range(1, groups):
            total += mm(x[g, :, lanes], aligned[g * rows : (g + 1) * rows, :], ((0,), (0,)))
        return total

    def share_copy(d):
        return pltpu.make_async_remote_copy(
            s_buf.at[d], s_in.at[d], s_send.at[d], s_recv.at[d],
            device_id={"fsdp": lax.rem(idx + d, shards)}, device_id_type=MESH,
        )

    @pl.loop(1, shards)
    def _(d):
        s_buf[d] = weight_share(d).astype(BF16)
        share_copy(d).start()

    def memory_part(target):
        start = pl.multiple_of(target * rows + seg_rows, 16)
        return mm(aligned[pl.ds(start, mem_rows), :], w[...], ((1,), (1,))).astype(BF16)

    def columns(block):
        return pl.ds(pl.multiple_of(block * depth + me * part, 128), part)

    for d in range(1, groups):
        m_buf[d] = memory_part(lax.rem(me + d, groups))
        for block in range(shards):
            to_group(
                d, m_buf.at[d, :, pl.ds(block * part, part)], gm_out.at[:, columns(block)],
                m_send, m_recv,
            ).start()
    m_buf[0] = memory_part(me)
    for block in range(shards):
        gm_out[:, columns(block)] = m_buf[0, :, block * part : (block + 1) * part]
    v_own[...] = value_part(0)
    s_own[...] = weight_share(0)

    total = v_own[...]
    for d in range(1, groups):
        value_copy(d).wait_recv()
        total += v_in[d]
    values[...] = total.astype(BF16)
    attention_backward(
        queries, all_keys, cotangent, values, lengths, gq_out, gk_out, mem_grads
    )
    k_in[me] = mem_grads[...]

    def key_copy(d):
        return to_group(d, mem_grads, k_in.at[me], k_send, k_recv)

    for d in range(1, groups):
        key_copy(d).start()

    @pl.loop(1, shards)
    def _(d):
        share_copy(d).wait_recv()
        s_own[...] += s_in[d].astype(F32)

    mine = pl.ds(pl.multiple_of(me * part, 16), part)
    gw_out[mine, :] = s_own[...].astype(BF16)

    def final_copy(d):
        return to_group(d, gw_out.at[mine], gw_out.at[mine], f_send, f_recv)

    for d in range(1, groups):
        final_copy(d).start()
    for d in range(1, groups):
        key_copy(d).wait_recv()
    for k in range(slots):
        gmk_out[k * mem_len : (k + 1) * mem_len, :] = k_in[
            dest[0, k], k * mem_len : (k + 1) * mem_len, :
        ]
    for d in range(1, groups):
        value_copy(d).wait_send()
        key_copy(d).wait_send()
        to_group(d, m_buf.at[d], m_buf.at[d], m_send, m_recv).wait()
        final_copy(d).wait()

    @pl.loop(1, shards)
    def _(d):
        share_copy(d).wait_send()


def run_tail(groups, shards, x, w, grads, queries, all_keys, cotangent, dest, lengths):
    slots, key_count, kv_width = all_keys.shape
    rows, width = x.shape[1:]
    seg_rows = queries.shape[0]
    mem_rows = rows - seg_rows
    part = width // shards
    vmem = pl.BlockSpec(memory_space=pltpu.VMEM)
    smem = pl.BlockSpec(memory_space=pltpu.SMEM)
    dma = pltpu.SemaphoreType.DMA
    return pl.pallas_call(
        tail_kernel,
        out_shape=(
            jax.ShapeDtypeStruct(queries.shape, BF16),
            jax.ShapeDtypeStruct((seg_rows, kv_width), BF16),
            jax.ShapeDtypeStruct((mem_rows, width * groups), BF16),
            jax.ShapeDtypeStruct((mem_rows, kv_width), BF16),
            jax.ShapeDtypeStruct((part * groups, kv_width), BF16),
        ),
        in_specs=[vmem] * 6 + [smem] * 2,
        out_specs=(vmem,) * 5,
        scratch_shapes=[
            pltpu.VMEM((groups * rows, kv_width), BF16),
            pltpu.VMEM((rows, width), BF16),
            pltpu.VMEM((rows, kv_width), F32),
            pltpu.VMEM((groups, rows, kv_width), F32),
            pltpu.VMEM((groups, rows, kv_width), F32),
            pltpu.VMEM((rows, kv_width), BF16),
            pltpu.VMEM((part, kv_width), F32),
            pltpu.VMEM((shards, part, kv_width), BF16),
            pltpu.VMEM((shards, part, kv_width), BF16),
            pltpu.VMEM((groups, mem_rows, width), BF16),
            pltpu.VMEM((mem_rows, kv_width), BF16),
            pltpu.VMEM((groups, mem_rows, kv_width), BF16),
            dma((groups,)), dma((groups,)), dma((shards,)), dma((shards,)), dma((groups,)),
            dma((groups,)), dma((groups,)), dma((groups,)), dma((groups,)), dma((groups,)),
        ],
        compiler_params=pltpu.CompilerParams(
            collective_id=1, has_side_effects=True, vmem_limit_bytes=48 * 2**20
        ),
        name="tail",
    )(x, w, grads, queries, all_keys, cotangent, dest, lengths)


def pick(table, rows):
    shape = table.T.shape + (1,) * (rows.ndim - 1)
    return jnp.sum(jnp.where(table.T.reshape(shape), rows[None], 0), axis=1, dtype=rows.dtype)


def take(table, blocks):
    shape = table.shape + (1,) * (blocks.ndim - 1)
    return jnp.sum(jnp.where(table.reshape(shape), blocks[None], 0), axis=1, dtype=blocks.dtype)


def rotate(blocks, shift):
    groups = blocks.shape[0]
    return lax.dynamic_slice_in_dim(
        jnp.concatenate([blocks, blocks], axis=0), groups - shift, groups, axis=0
    )


def swap(blocks):
    return lax.all_to_all(blocks, "dp", split_axis=0, concat_axis=0, tiled=True)


def softmax_part(query_heads, all_keys, masked):
    seg_len = query_heads.shape[0]
    key_count = all_keys.shape[0]
    mem_len = key_count - seg_len
    scores = jnp.einsum("qkgd,jkd->kgqj", query_heads, all_keys, preferred_element_type=F32) * SCALE
    positions = jnp.arange(seg_len)[:, None]
    columns = jnp.arange(key_count)[None, :]
    visible = (columns < mem_len) | (columns - mem_len <= positions)
    scores = jnp.where(visible, scores, -1e30)
    row_max = jnp.max(scores, axis=-1, keepdims=True)
    exp_scores = jnp.exp(scores - row_max)
    weights = exp_scores / jnp.sum(exp_scores, axis=-1, keepdims=True)
    weights_low = weights.astype(BF16)
    grad_values = jnp.einsum("kgqj,qkgd->jkd", weights_low, masked, preferred_element_type=F32)
    return weights, weights_low, grad_values.reshape(key_count, -1).astype(BF16)


def plain_forward(
    groups, shards, tokens, memory, weight, mem_keys, queries, keys, cotangent,
    send_table, take_table, lengths,
):
    me = lax.axis_index("dp")
    slots = lengths.shape[1]
    seg_rows, mem_rows = tokens.shape[0], memory.shape[0]
    rows = seg_rows + mem_rows
    seg_len, mem_len = seg_rows // slots, mem_rows // slots
    depth, kv_width = weight.shape
    part = depth // groups
    heads_kv = kv_width // HEAD_DIM
    group_size = queries.shape[1] // kv_width
    in_keys = swap(pick(send_table, mem_keys.reshape(slots, mem_len, kv_width)))
    weight_part = lax.all_gather(
        lax.dynamic_slice_in_dim(weight, me * part, part, axis=0), "fsdp", axis=0, tiled=True
    )
    stacked = jnp.concatenate([tokens, memory], axis=0)
    stacked = stacked.reshape(rows, shards, groups, part).transpose(2, 0, 1, 3)
    stacked = swap(stacked.reshape(groups, rows, shards * part))

    slot_keys = take(take_table, in_keys)
    all_keys = jnp.concatenate([slot_keys, keys.reshape(slots, seg_len, kv_width)], axis=1)
    all_keys = all_keys.reshape(slots, mem_len + seg_len, heads_kv, HEAD_DIM)
    query_heads = queries.reshape(slots, seg_len, heads_kv, group_size, HEAD_DIM)
    live = (jnp.arange(seg_len)[None, :] < lengths[0][:, None]).astype(BF16)
    masked = cotangent.reshape(query_heads.shape) * live[:, :, None, None, None]
    weights, weights_low, grad_values = jax.vmap(softmax_part)(query_heads, all_keys, masked)

    own_grads = jnp.concatenate(
        [
            grad_values[:, mem_len:].reshape(seg_rows, kv_width),
            grad_values[:, :mem_len].reshape(mem_rows, kv_width),
        ],
        axis=0,
    )
    peer_grads = swap(jnp.broadcast_to(own_grads[None], (groups, rows, kv_width)))
    return stacked, weight_part, peer_grads, all_keys.reshape(slots, -1, kv_width)


def per_device(
    tokens, queries, keys, memory, mem_keys, cotangent, value_weight, dest_group, source_group, lengths
):
    groups = lax.axis_size("dp")
    shards = lax.axis_size("fsdp")
    me = lax.axis_index("dp")
    slots = dest_group.shape[1]
    seg_len = tokens.shape[1] // slots
    mem_len = memory.shape[1] // slots
    kv_width = value_weight.shape[1]
    width = tokens.shape[2]
    part = value_weight.shape[0] // groups
    seg_rows, mem_rows = slots * seg_len, slots * mem_len
    rows = seg_rows + mem_rows
    targets = jnp.arange(groups, dtype=jnp.int32)
    send_table = dest_group[0][:, None] == targets[None, :]
    take_table = source_group[0][:, None] == targets[None, :]
    shift = lax.rem(dest_group[0] - me + groups, groups)

    arrays = (tokens[0], memory[0], value_weight, mem_keys[0], queries[0], keys[0], cotangent[0])
    if part % 128:
        forward = plain_forward(groups, shards, *arrays, send_table, take_table, lengths)
    else:
        stacked, weight_part, peer_grads, all_keys = run_forward(
            groups, shards, *arrays, source_group, lengths
        )
        results = run_tail(
            groups, shards, stacked, weight_part, peer_grads, queries[0], all_keys, cotangent[0],
            dest_group, lengths,
        )
        return tuple(result[None] for result in results[:4]) + (results[4],)
    stacked, weight_part, peer_grads, all_keys = forward
    doc_grads = [
        rotate(
            peer_grads[:, seg_rows + k * mem_len : seg_rows + (k + 1) * mem_len],
            lax.rem(groups - shift[k], groups),
        )
        for k in range(slots)
    ]
    doc_grads = jnp.concatenate(doc_grads, axis=1)
    all_grads = jnp.concatenate([peer_grads[:, :seg_rows], doc_grads], axis=1)
    share = lax.dot_general(
        stacked.reshape(groups * rows, shards * part),
        all_grads.reshape(groups * rows, kv_width),
        (((0,), (0,)), ((), ())),
        preferred_element_type=F32,
    ).astype(BF16)
    share = lax.psum_scatter(share, "fsdp", scatter_dimension=0, tiled=True)
    grad_weight = lax.all_gather(share, "dp", axis=0, tiled=True)

    partial = jnp.dot(
        stacked.reshape(groups * rows, shards * part), weight_part, preferred_element_type=F32
    ).reshape(groups, rows, kv_width)
    routed = [partial[:, :seg_rows]] + [
        rotate(partial[:, seg_rows + k * mem_len : seg_rows + (k + 1) * mem_len], shift[k])
        for k in range(slots)
    ]
    values = jnp.sum(swap(jnp.concatenate(routed, axis=1)), axis=0).astype(BF16)
    grad_query, grad_keys, slot_grad_keys = run_backward(queries[0], all_keys, cotangent[0], values, lengths)
    doc_grad_keys = take(send_table, swap(pick(take_table, slot_grad_keys.reshape(slots, mem_len, kv_width))))

    grad_memory = lax.dot_general(
        doc_grads.reshape(groups * mem_rows, kv_width),
        weight_part,
        (((1,), (1,)), ((), ())),
        preferred_element_type=F32,
    ).astype(BF16)
    grad_memory = swap(grad_memory.reshape(groups, mem_rows, shards * part))
    grad_memory = grad_memory.reshape(groups, mem_rows, shards, part).transpose(1, 2, 0, 3)
    return (
        grad_query[None],
        grad_keys[None],
        grad_memory.reshape(1, mem_rows, width),
        doc_grad_keys.reshape(1, mem_rows, kv_width),
        grad_weight,
    )


def solution(mesh):
    rows = P("dp", "fsdp", None)
    table = P("dp", "fsdp")
    weight = P("fsdp", None)
    return jax.shard_map(
        per_device,
        mesh=mesh,
        in_specs=(rows,) * 6 + (weight, table, table, table),
        out_specs=(rows,) * 4 + (weight,),
        check_vma=False,
    )
```
